1024 devices in a mesh: dp: 16 (over y, x), expert: 64 (over z, core).
Axes of the slice: x: 4, y: 4, z: 32, core: 2. Of those that a mesh axis runs over, the one named last changes fastest.
Arguments:
- tokens: bfloat16 [8192, 3584], P('expert'), may hold values from -6 to 6
- up_saved: bfloat16 [8192, 8, 2048], P('expert', None, 'dp'), may hold values from -6 to 6
- hidden_grad: bfloat16 [8192, 8, 2048], P('expert', None, 'dp'), may hold values from -1.5 to 1.5
- route_device: int32 [8192, 8], P('expert'), may hold values from 0 to 255, as said below
- on_replica: int32 [64, 64], replicated, may hold values from 0 to 1, as said below
- gate_weight: bfloat16 [64, 3584, 2048], P('expert', None, 'dp'), may hold values from -0.09375 to 0.09375
Outputs:
- token_grad: bfloat16 [8192, 3584], P('expert', 'dp')
- gate_grad: bfloat16 [64, 3584, 2048], P('expert', None, 'dp')
The draws below stay inside these ranges and needn't reach their ends.
Inputs may be any that keep to these rules, and one draw needn't show every extreme that they name: `route_device`: each token names 8 different numbers. In each aligned block of 128 tokens (those of one index of expert) every number that the block names is named by exactly 4 tokens. Numbers under 64 are devices along expert; device n holds expert n and a replica of expert (n + 32) mod 64. For every device n along expert, some block of tokens that names n has on_replica 1 for n.
All inputs are finite; a program needn't handle non-finite values.
Results may differ from the reference program's by a relative error of at most 0.022.
Values may be sent and summed in bfloat16 or wider, within the bound.
A program may use at most 32 MiB of HBM per device.

```python
import jax
import jax.numpy as jnp
from jax import lax

D = 3584
FF = 2048
TOPK = 8
EXPERTS_ALL = 256
CAP = 4
TOK_DEV = 128
TOKENS = 8192
N_DP = 16
N_EXPERT = 64


def shift_of(key):
    return jax.random.randint(jax.random.fold_in(key, 5), (), 0, N_EXPERT).astype(jnp.int32)


def named_span():
    return min(TOK_DEV * TOPK // CAP // 2, N_EXPERT)


def draw_route_device(key, part):
    offset_all = shift_of(key)
    key = jax.random.fold_in(key, 11)
    blocks = TOKENS // TOK_DEV
    used = TOK_DEV * TOPK // CAP
    per_round = used // TOPK
    span = named_span()

    def one_block(block_key, block_index):
        keys = jax.random.split(block_key, 4)
        offsets = jax.random.randint(keys[0], (CAP,), 0, used).astype(jnp.int32)
        devices = ((offset_all + block_index * span + jnp.arange(span, dtype=jnp.int32)) % N_EXPERT).astype(jnp.int32)
        outside = (N_EXPERT + jax.random.permutation(keys[3], EXPERTS_ALL - N_EXPERT)[:used - span]).astype(jnp.int32)
        pool = jnp.concatenate([devices, outside], axis=0)
        labels = pool[jax.random.permutation(keys[1], used)].astype(jnp.int32)
        order = jax.random.permutation(keys[2], TOK_DEV).astype(jnp.int32)
        token_ids = jnp.arange(TOK_DEV, dtype=jnp.int32)
        start = token_ids % per_round * TOPK + offsets[token_ids // per_round]
        index = ((start[:, None] + jnp.arange(TOPK, dtype=jnp.int32)[None, :]) % used).astype(jnp.int32)
        listing = labels[index]
        return listing[order]
    block_keys = jax.random.split(key, blocks)
    listed = jax.vmap(one_block)(block_keys, jnp.arange(blocks, dtype=jnp.int32))
    return listed.reshape(TOKENS, TOPK).astype(jnp.int32)


def draw_on_replica(key, part):
    offset_all = shift_of(key)
    key = jax.random.fold_in(key, 23)
    span = named_span()
    base = (jax.random.randint(key, (N_EXPERT, N_EXPERT), 0, 3) == 0).astype(jnp.int32)
    columns = jnp.arange(N_EXPERT, dtype=jnp.int32)
    chosen = ((columns - offset_all) % N_EXPERT // span).astype(jnp.int32)
    forced = (jnp.arange(N_EXPERT, dtype=jnp.int32)[:, None] == chosen[None, :]).astype(jnp.int32)
    return jnp.maximum(base, forced).astype(jnp.int32)


def block_levels(rng, extent, cuts, least, top_value):
    def one(dim, blocks):
        draws = jax.random.uniform(jax.random.fold_in(jax.random.fold_in(rng, 6), dim), (blocks,), jnp.float32, least / len(cuts), top_value / len(cuts))
        return jnp.repeat(jnp.exp(draws), extent[dim] // blocks).reshape((-1,) + (1,) * (len(extent) - dim - 1))

    loudness = one(*cuts[0])
    for cut in cuts[1:]:
        loudness = loudness * one(*cut)
    return loudness


def noise(key, shape, scale, reach, shards=(), held_as=jnp.bfloat16):
    gain = block_levels(key, shape, shards, -0.22, 0.18) if shards else 1.0
    drawn = jax.random.normal(key, shape, jnp.float32) * scale * gain
    return jnp.minimum(jnp.maximum(drawn, -reach), reach).astype(held_as)


def setup_inputs(seed: int = 0) -> dict:
    key_of = jax.random.split(jax.random.key(seed), 7)
    tokens = noise(key_of[0], (TOKENS, D), 1.0, 6.0, ((0, 64),))
    up_saved = noise(key_of[1], (TOKENS, TOPK, FF), 1.0, 6.0, ((0, 64), (2, 16)))
    hidden_grad = noise(key_of[2], (TOKENS, TOPK, FF), 0.25, 1.5, ((0, 64), (2, 16)))
    route_device = draw_route_device(jax.random.fold_in(key_of[6], 71), 0)
    on_replica = draw_on_replica(jax.random.fold_in(key_of[6], 71), 0)
    gate_weight = noise(key_of[5], (N_EXPERT, D, FF), D ** -0.5, 0.09375, ((0, 64), (2, 16)))
    return dict(tokens=tokens, up_saved=up_saved, hidden_grad=hidden_grad, route_device=route_device, on_replica=on_replica, gate_weight=gate_weight)


def gate_delta_of(gate_value, grad_rows, up_rows):
    logistic = jax.nn.sigmoid(gate_value)
    slope = logistic * (1.0 + gate_value * (1.0 - logistic))
    return (grad_rows.astype(jnp.float32) * up_rows.astype(jnp.float32) * slope).astype(jnp.bfloat16)


def reference(tokens, up_saved, hidden_grad, route_device, on_replica, gate_weight):
    halfway = N_EXPERT // 2
    per_block = TOK_DEV * TOPK
    dump = N_EXPERT * CAP
    routes = route_device.reshape(N_EXPERT, per_block)
    inside = routes < N_EXPERT
    onehot = (routes[:, :, None] == jnp.arange(N_EXPERT, dtype=jnp.int32)[None, None, :]).astype(jnp.int32)
    earlier = jnp.cumsum(onehot, axis=1) - onehot
    position = jnp.sum(earlier * onehot, axis=2)
    slot_of = jnp.where(inside, routes * CAP + position, dump).astype(jnp.int32)
    block_ids = jnp.arange(N_EXPERT, dtype=jnp.int32)[:, None] * jnp.ones((1, per_block), jnp.int32)
    route_ids = jnp.ones((N_EXPERT, 1), jnp.int32) * jnp.arange(per_block, dtype=jnp.int32)[None, :]
    slot_table = jnp.full((N_EXPERT, dump + 1), -1, jnp.int32).at[block_ids, slot_of].set(route_ids)
    slot_table = slot_table[:, :dump].reshape(N_EXPERT, N_EXPERT, CAP)
    token_blocks = tokens.reshape(N_EXPERT, TOK_DEV, D)
    grad_blocks = hidden_grad.reshape(N_EXPERT, per_block, FF)
    up_blocks = up_saved.reshape(N_EXPERT, per_block, FF)

    def gather_rows(device, flag_value):
        entries = jnp.take(slot_table, device, axis=1)
        flags = jnp.take(on_replica, device, axis=1)
        active = (entries >= 0) & (flags[:, None] == flag_value)
        safe_index = jnp.maximum(entries, 0).astype(jnp.int32)
        rows = jnp.take_along_axis(token_blocks, (safe_index // TOPK)[:, :, None], axis=1)
        grads = jnp.take_along_axis(grad_blocks, safe_index[:, :, None], axis=1)
        ups = jnp.take_along_axis(up_blocks, safe_index[:, :, None], axis=1)
        keep = active[:, :, None]
        nothing = jnp.zeros((), tokens.dtype)
        return (jnp.where(keep, rows, nothing).reshape(-1, D),
                jnp.where(keep, grads, nothing).reshape(-1, FF),
                jnp.where(keep, ups, nothing).reshape(-1, FF))

    def per_expert(expert_index):
        partner = (expert_index + halfway) % N_EXPERT
        own_rows, own_grads, own_ups = gather_rows(expert_index, 0)
        rep_rows, rep_grads, rep_ups = gather_rows(partner, 1)
        count = own_rows.shape[0]
        rows_all = jnp.concatenate([own_rows, rep_rows], axis=0)
        weight = jnp.take(gate_weight, expert_index, axis=0)
        gate_value = jnp.dot(rows_all, weight, preferred_element_type=jnp.float32)
        gate_delta = gate_delta_of(gate_value, jnp.concatenate([own_grads, rep_grads], axis=0),
                                   jnp.concatenate([own_ups, rep_ups], axis=0))
        home_grad = jnp.dot(own_rows.T, gate_delta[:count], preferred_element_type=jnp.float32)
        replica_grad = jnp.dot(rep_rows.T, gate_delta[count:], preferred_element_type=jnp.float32).astype(jnp.bfloat16)
        weight_grad = (home_grad + replica_grad.astype(jnp.float32)).astype(jnp.bfloat16)
        blocked_delta = gate_delta.astype(jnp.float32).reshape(-1, N_DP, FF // N_DP)
        blocked_weight = weight.astype(jnp.float32).reshape(D, N_DP, FF // N_DP)
        terms = jnp.einsum("rbh,dbh->rbd", blocked_delta, blocked_weight).astype(jnp.bfloat16)
        route_grad = jnp.sum(terms.astype(jnp.float32), axis=1).astype(jnp.bfloat16)
        return (weight_grad, route_grad[:count].reshape(N_EXPERT, CAP, D),
                route_grad[count:].reshape(N_EXPERT, CAP, D))

    gate_grad, own_terms, rep_terms = lax.map(per_expert, jnp.arange(N_EXPERT, dtype=jnp.int32))
    slot_grad = own_terms.astype(jnp.float32) + jnp.roll(rep_terms, halfway, axis=0).astype(jnp.float32)
    by_block = jnp.transpose(slot_grad, (1, 0, 2, 3)).reshape(N_EXPERT, dump, D)
    owner = jnp.where(slot_table >= 0, slot_table // TOPK, TOK_DEV).reshape(N_EXPERT, dump).astype(jnp.int32)
    block_index = jnp.arange(N_EXPERT, dtype=jnp.int32)[:, None] * jnp.ones((1, dump), jnp.int32)
    sums = jnp.zeros((N_EXPERT, TOK_DEV + 1, D), jnp.float32).at[block_index, owner].add(by_block)
    token_grad = sums[:, :TOK_DEV].reshape(TOKENS, D).astype(jnp.bfloat16)
    return token_grad, gate_grad
```

```python
import functools

import jax
import jax.numpy as jnp
from jax import lax
from jax.experimental import pallas as pl
from jax.experimental.pallas import tpu as pltpu
from jax.sharding import PartitionSpec as P

CAP = 4
SLOTS = 2 * CAP
PAIR = 2 * SLOTS
MESH = pl.DeviceIdType.MESH
F32 = jnp.float32
BF16 = jnp.bfloat16


def dot(a, b, contract=((1,), (0,))):
    return lax.dot_general(a, b, (contract, ((), ())), preferred_element_type=F32)


def await_bytes(view, sem):
    pltpu.make_async_copy(view, view, sem).wait()


def kernel(
    parts,
    chips,
    share,
    tok_ref,
    prod_ref,
    route_ref,
    flag_ref,
    weight_ref,
    token_out,
    weight_out,
    pick,
    own_rows,
    own_aux,
    away_rows,
    away_aux,
    twin_rows,
    twin_aux,
    rows,
    aux,
    wide,
    partial,
    terms,
    delta,
    back,
    ret,
    twin_ret,
    grads,
    send_sems,
    recv_sems,
):
    experts = 2 * chips
    halfway = experts // 2
    slots = chips * PAIR
    tokens = tok_ref.shape[0]
    hidden = prod_ref.shape[2]
    routes = prod_ref.shape[0]
    part = lax.axis_index("dp")
    place = lax.axis_index("expert")
    chip = place // 2
    core = place % 2
    twin = (part, chip * 2 + 1 - core)

    def far(step):
        return (part, lax.rem(chip + step, chips) * 2 + core)

    def beside(step):
        return (lax.rem(part + step, parts), place)

    barrier = pltpu.get_barrier_semaphore()

    def greet(device):
        pl.semaphore_signal(barrier, inc=1, device_id=device, device_id_type=MESH)

    greet(twin)

    @pl.loop(1, chips)
    def _(step):
        greet(far(step))

    @pl.loop(1, parts)
    def _(step):
        greet(beside(step))

    wide[pl.ds(share, wide.shape[0] - share), :] = jnp.zeros(
        (wide.shape[0] - share, wide.shape[1]), BF16
    )

    named = route_ref[...]
    numbers = lax.broadcasted_iota(jnp.int32, (experts, tokens), 0)
    count = jnp.zeros((experts, tokens), F32)
    for k in range(routes):
        count = count + jnp.where(named[k : k + 1, :] == numbers, 1.0, 0.0)
    before = lax.broadcasted_iota(jnp.int32, (tokens, tokens), 0)
    after = lax.broadcasted_iota(jnp.int32, (tokens, tokens), 1)
    earlier = dot(count.astype(BF16), jnp.where(before < after, 1.0, 0.0).astype(BF16))
    flags = flag_ref[...].astype(F32)
    target = []
    for k in range(routes):
        here = named[k : k + 1, :] == numbers
        position = jnp.sum(jnp.where(here, earlier, 0.0), axis=0, keepdims=True).astype(jnp.int32)
        flag = jnp.sum(jnp.where(here, flags, 0.0), axis=0, keepdims=True).astype(jnp.int32)
        number = named[k : k + 1, :]
        server = lax.rem(number + flag * halfway, experts)
        row = (server // 2) * PAIR + core * SLOTS + flag * CAP + position
        target.append((jnp.where(number < experts, row, -1), lax.rem(server, 2)))

    row_ids = lax.broadcasted_iota(jnp.int32, (slots, tokens), 0)

    def fill(side, rows_ref, aux_ref):
        total = jnp.zeros((slots, hidden), F32)
        every = jnp.zeros((slots, tokens), F32)
        for k in range(routes):
            row, parity = target[k]
            chosen = jnp.where(row_ids == jnp.where(parity == side, row, -1), 1.0, 0.0)
            every = every + chosen
            total = total + dot(chosen.astype(BF16), prod_ref[k])
        matrix = every.astype(BF16)
        rows_ref[...] = dot(matrix, tok_ref[...]).astype(BF16)
        aux_ref[...] = total.astype(BF16)
        return matrix

    pick[1] = fill(1 - core, away_rows, away_aux)

    pl.semaphore_wait(barrier, 1 + (chips - 1) + (parts - 1))

    def remote(src, dst, sem, device):
        copy = pltpu.make_async_remote_copy(
            src_ref=src,
            dst_ref=dst,
            send_sem=send_sems.at[sem],
            recv_sem=recv_sems.at[sem],
            device_id=device,
            device_id_type=MESH,
        )
        copy.start()

    remote(away_rows, twin_rows, 0, twin)
    remote(away_aux, twin_aux, 1, twin)

    own_columns = pl.ds(pl.multiple_of(part * hidden, hidden), hidden)

    @pl.loop(1, parts)
    def _(step):
        other = lax.rem(part + step, parts)
        remote(
            weight_ref.at[pl.ds(pl.multiple_of(other * share, 16), share)],
            wide.at[pl.ds(0, share), own_columns],
            2,
            (other, place),
        )

    wide[pl.ds(0, share), own_columns] = weight_ref[
        pl.ds(pl.multiple_of(part * share, 16), share), :
    ]
    pick[0] = fill(core, own_rows, own_aux)

    await_bytes(twin_rows, recv_sems.at[0])
    own_rows[...] = own_rows[...] + twin_rows[...]

    def sixteen(index):
        return pl.ds(pl.multiple_of(index * PAIR, PAIR), PAIR)

    @pl.loop(1, chips)
    def _(step):
        other = lax.rem(chip + step, chips)
        remote(own_rows.at[sixteen(other)], rows.at[sixteen(chips - step)], 3, far(step))

    rows[pl.ds(0, PAIR), :] = own_rows[sixteen(chip), :]
    await_bytes(twin_aux, recv_sems.at[1])
    own_aux[...] = own_aux[...] + twin_aux[...]

    @pl.loop(1, chips)
    def _(step):
        other = lax.rem(chip + step, chips)
        remote(own_aux.at[sixteen(other)], aux.at[sixteen(chips - step)], 4, far(step))

    aux[pl.ds(0, PAIR), :] = own_aux[sixteen(chip), :]

    few = (parts - 1) * share
    await_bytes(weight_ref.at[pl.ds(0, few)], recv_sems.at[2])
    most = pl.ds(0, (chips - 1) * PAIR)
    await_bytes(rows.at[most], recv_sems.at[3])

    for j in range(0, parts, 2):
        two = dot(rows[...], wide[:, j * hidden : (j + 2) * hidden]).astype(BF16)
        partial[j] = two[:, :hidden]
        partial[j + 1] = two[:, hidden:]

    @pl.loop(1, parts)
    def _(step):
        other = lax.rem(part + step, parts)
        remote(partial.at[other], terms.at[part], 5, (other, place))

    terms[part] = partial[part]
    await_bytes(terms.at[pl.ds(0, parts - 1)], recv_sems.at[5])
    gate = terms[0].astype(F32)
    for i in range(1, parts):
        gate = gate + terms[i].astype(F32)
    await_bytes(aux.at[most], recv_sems.at[4])
    logistic = jax.nn.sigmoid(gate)
    slope = logistic * (1.0 + gate * (1.0 - logistic))
    delta[:, own_columns] = (aux[...].astype(F32) * slope).astype(BF16)

    @pl.loop(1, parts)
    def _(step):
        remote(delta.at[:, own_columns], delta.at[:, own_columns], 6, beside(step))

    await_bytes(terms.at[pl.ds(0, parts - 1)], recv_sems.at[6])
    back[...] = dot(delta[...], wide[...], ((1,), (1,))).astype(BF16)

    @pl.loop(1, chips)
    def _(step):
        remote(back.at[sixteen(step)], ret.at[sixteen(chip)], 7, far(step))

    ret[sixteen(chip), :] = back[pl.ds(0, PAIR), :]

    rows_turned = rows[...].T
    for j in range(0, parts, 2):
        two = dot(rows_turned, delta[:, j * hidden : (j + 2) * hidden]).astype(BF16)
        grads[j] = two[:share, :hidden]
        grads[j + 1] = two[:share, hidden:]

    own_share = pl.ds(pl.multiple_of(part * share, 16), share)

    @pl.loop(1, parts)
    def _(step):
        other = lax.rem(part + step, parts)
        remote(grads.at[other], weight_out.at[own_share], 8, (other, place))

    weight_out[own_share, :] = grads[part]

    await_bytes(ret.at[most], recv_sems.at[7])
    remote(ret, twin_ret, 9, twin)
    total = dot(pick[0], ret[...], ((0,), (0,)))
    await_bytes(twin_ret, recv_sems.at[9])
    total = total + dot(pick[1], twin_ret[...], ((0,), (0,)))
    token_out[...] = total[:, :share].astype(BF16)

    await_bytes(weight_out.at[pl.ds(0, few)], recv_sems.at[8])

    await_bytes(away_rows, send_sems.at[0])
    await_bytes(away_aux, send_sems.at[1])
    await_bytes(weight_ref.at[pl.ds(0, few)], send_sems.at[2])
    await_bytes(own_rows.at[most], send_sems.at[3])
    await_bytes(own_aux.at[most], send_sems.at[4])
    await_bytes(partial.at[pl.ds(0, parts - 1)], send_sems.at[5])
    await_bytes(partial.at[pl.ds(0, parts - 1)], send_sems.at[6])
    await_bytes(back.at[most], send_sems.at[7])
    await_bytes(weight_out.at[pl.ds(0, few)], send_sems.at[8])
    await_bytes(ret, send_sems.at[9])


def local(tokens, up_saved, hidden_grad, route_device, on_replica, gate_weight):
    experts = lax.axis_size("expert")
    parts = lax.axis_size("dp")
    part = lax.axis_index("dp")
    place = lax.axis_index("expert")
    chips = experts // 2
    tok_count, routes = route_device.shape
    width = tokens.shape[1]
    share = width // parts
    padded = -(-share // 128) * 128
    hidden = gate_weight.shape[2]
    slots = chips * PAIR
    tok = lax.dynamic_slice_in_dim(tokens, part * share, share, 1)
    tok = jnp.pad(tok, ((0, 0), (0, padded - share)))
    prod = (hidden_grad.astype(F32) * up_saved.astype(F32)).astype(BF16).transpose(1, 0, 2)
    flag = lax.dynamic_slice_in_dim(on_replica, place, 1, 0).reshape(experts, 1)
    vmem = pl.BlockSpec(memory_space=pltpu.VMEM)
    return pl.pallas_call(
        functools.partial(kernel, parts, chips, share),
        out_shape=(
            jax.ShapeDtypeStruct((tok_count, share), BF16),
            jax.ShapeDtypeStruct((width, hidden), BF16),
        ),
        in_specs=[vmem] * 5,
        out_specs=(vmem, vmem),
        scratch_shapes=[
            pltpu.VMEM((2, slots, tok_count), BF16),
            pltpu.VMEM((slots, padded), BF16),
            pltpu.VMEM((slots, hidden), BF16),
            pltpu.VMEM((slots, padded), BF16),
            pltpu.VMEM((slots, hidden), BF16),
            pltpu.VMEM((slots, padded), BF16),
            pltpu.VMEM((slots, hidden), BF16),
            pltpu.VMEM((slots, padded), BF16),
            pltpu.VMEM((slots, hidden), BF16),
            pltpu.VMEM((padded, parts * hidden), BF16),
            pltpu.VMEM((parts, slots, hidden), BF16),
            pltpu.VMEM((parts, slots, hidden), BF16),
            pltpu.VMEM((slots, parts * hidden), BF16),
            pltpu.VMEM((slots, padded), BF16),
            pltpu.VMEM((slots, padded), BF16),
            pltpu.VMEM((slots, padded), BF16),
            pltpu.VMEM((parts, share, hidden), BF16),
            pltpu.SemaphoreType.DMA((10,)),
            pltpu.SemaphoreType.DMA((10,)),
        ],
        compiler_params=pltpu.CompilerParams(
            collective_id=0, has_side_effects=True, vmem_limit_bytes=48 * 1024 * 1024
        ),
        cost_estimate=pl.CostEstimate(
            flops=6 * slots * padded * parts * hidden, bytes_accessed=4 << 20, transcendentals=0
        ),
    )(tok, prod, route_device.T, flag, gate_weight[0])


def solution(mesh):
    placed = (
        P("expert", None),
        P("expert", None, "dp"),
        P("expert", None, "dp"),
        P("expert", None),
        P(),
        P("expert", None, "dp"),
    )

    def whole(*args):
        token_grad, gate_grad = local(*args)
        return token_grad, gate_grad[None]

    return jax.shard_map(
        whole,
        mesh=mesh,
        in_specs=placed,
        out_specs=(P("expert", "dp"), P("expert", None, "dp")),
        check_vma=False,
    )
```

```python
import functools
import math

import jax
import jax.numpy as jnp
from jax import lax
from jax.experimental import pallas as pl
from jax.experimental.pallas import tpu as pltpu
from jax.sharding import PartitionSpec as P

CAP = 4
SLOTS = 2 * CAP
PAIR = 2 * SLOTS
BATCHES = 4
MESH = pl.DeviceIdType.MESH
F32 = jnp.float32
BF16 = jnp.bfloat16


def dot(a, b, contract=((1,), (0,))):
    return lax.dot_general(a, b, (contract, ((), ())), preferred_element_type=F32)


def await_bytes(view, sem):
    pltpu.make_async_copy(view, view, sem).wait()


def kernel(
    parts,
    chips,
    share,
    tok_ref,
    prod_ref,
    route_ref,
    flag_ref,
    weight_ref,
    token_out,
    weight_out,
    pick,
    own_rows,
    own_aux,
    away_rows,
    away_aux,
    twin_rows,
    twin_aux,
    rows,
    aux,
    wide,
    partial,
    first_terms,
    half_sums,
    second_terms,
    delta,
    back,
    ret,
    twin_ret,
    totals,
    grads,
    send_sems,
    recv_sems,
):
    experts = 2 * chips
    halfway = experts // 2
    slots = chips * PAIR
    near = chips // BATCHES
    size = slots // BATCHES
    half = size // 2
    edge = half_sums.shape[2]
    tokens = tok_ref.shape[0]
    hidden = prod_ref.shape[2]
    routes = prod_ref.shape[0]
    part = lax.axis_index("dp")
    place = lax.axis_index("expert")
    line, spot = part // edge, part % edge
    chip = place // 2
    core = place % 2
    twin = (part, chip * 2 + 1 - core)
    first, second = pl.ds(0, half), pl.ds(half, half)

    def ahead(step):
        return (part, lax.rem(chip + step, chips) * 2 + core)

    def behind(step):
        return (part, lax.rem(chip + chips - step, chips) * 2 + core)

    def along(step):
        return lax.rem(spot + step, edge)

    def across(step):
        return lax.rem(line + step, edge)

    barrier = pltpu.get_barrier_semaphore()

    def greet(device):
        pl.semaphore_signal(barrier, inc=1, device_id=device, device_id_type=MESH)

    greet(twin)

    @pl.loop(1, chips)
    def _(step):
        greet(ahead(step))

    @pl.loop(1, parts)
    def _(step):
        greet((lax.rem(part + step, parts), place))

    wide[pl.ds(share, wide.shape[0] - share), :] = jnp.zeros(
        (wide.shape[0] - share, wide.shape[1]), BF16
    )

    named = route_ref[...]
    numbers = lax.broadcasted_iota(jnp.int32, (experts, tokens), 0)
    count = jnp.zeros((experts, tokens), F32)
    for k in range(routes):
        count = count + jnp.where(named[k : k + 1, :] == numbers, 1.0, 0.0)
    before = lax.broadcasted_iota(jnp.int32, (tokens, tokens), 0)
    after = lax.broadcasted_iota(jnp.int32, (tokens, tokens), 1)
    earlier = dot(count.astype(BF16), jnp.where(before < after, 1.0, 0.0).astype(BF16))
    flags = flag_ref[...].astype(F32)
    target = []
    for k in range(routes):
        here = named[k : k + 1, :] == numbers
        position = jnp.sum(jnp.where(here, earlier, 0.0), axis=0, keepdims=True).astype(jnp.int32)
        flag = jnp.sum(jnp.where(here, flags, 0.0), axis=0, keepdims=True).astype(jnp.int32)
        number = named[k : k + 1, :]
        server = lax.rem(number + flag * halfway, experts)
        step = lax.rem(chip + chips - server // 2, chips)
        order = lax.rem(step, BATCHES) * near + step // BATCHES
        row = order * PAIR + core * SLOTS + flag * CAP + position
        target.append((jnp.where(number < experts, row, -1), lax.rem(server, 2)))

    row_ids = lax.broadcasted_iota(jnp.int32, (slots, tokens), 0)

    def fill(side, rows_ref, aux_ref):
        total = jnp.zeros((slots, hidden), F32)
        every = jnp.zeros((slots, tokens), F32)
        for k in range(routes):
            row, parity = target[k]
            chosen = jnp.where(row_ids == jnp.where(parity == side, row, -1), 1.0, 0.0)
            every = every + chosen
            total = total + dot(chosen.astype(BF16), prod_ref[k])
        matrix = every.astype(BF16)
        rows_ref[...] = dot(matrix, tok_ref[...]).astype(BF16)
        aux_ref[...] = total.astype(BF16)
        return matrix

    pick[1] = fill(1 - core, away_rows, away_aux)
    pl.semaphore_wait(barrier, 1 + (chips - 1) + (parts - 1))

    def remote(src, dst, sem, device):
        copy = pltpu.make_async_remote_copy(
            src_ref=src,
            dst_ref=dst,
            send_sem=send_sems.at[sem],
            recv_sem=recv_sems.at[sem],
            device_id=device,
            device_id_type=MESH,
        )
        copy.start()

    twin_rows_sem, twin_aux_sem, weight_sem, grad_sem = range(4)
    rows_sem, aux_sem, first_sem, second_sem, third_sem, fourth_sem, ret_sem, twin_sem = (
        4 + BATCHES * i for i in range(8)
    )

    remote(away_rows, twin_rows, twin_rows_sem, twin)
    remote(away_aux, twin_aux, twin_aux_sem, twin)

    own_columns = pl.ds(pl.multiple_of(part * hidden, hidden), hidden)

    @pl.loop(1, parts)
    def _(step):
        other = lax.rem(part + step, parts)
        remote(
            weight_ref.at[pl.ds(pl.multiple_of(other * share, 16), share)],
            wide.at[pl.ds(0, share), own_columns],
            weight_sem,
            (other, place),
        )

    wide[pl.ds(0, share), own_columns] = weight_ref[
        pl.ds(pl.multiple_of(part * share, 16), share), :
    ]
    pick[0] = fill(core, own_rows, own_aux)

    def group(index):
        return pl.ds(pl.multiple_of(index * PAIR, PAIR), PAIR)

    def arrived(batch):
        lowest = batch * size + (PAIR if batch == 0 else 0)
        return pl.ds(lowest, (batch + 1) * size - lowest)

    def spread(batch, src, dst, sem, device_of):
        @pl.loop(1 if batch == 0 else 0, near)
        def _(index):
            where = group(batch * near + index)
            remote(src.at[where], dst.at[where], sem + batch, device_of(index * BATCHES + batch))

        if batch == 0:
            dst[pl.ds(0, PAIR), :] = src[pl.ds(0, PAIR), :]

    await_bytes(twin_rows, recv_sems.at[twin_rows_sem])
    own_rows[...] = own_rows[...] + twin_rows[...]
    spread(0, own_rows, rows, rows_sem, behind)
    await_bytes(twin_aux, recv_sems.at[twin_aux_sem])
    own_aux[...] = own_aux[...] + twin_aux[...]
    spread(0, own_aux, aux, aux_sem, behind)
    for batch in range(1, BATCHES):
        spread(batch, own_rows, rows, rows_sem, behind)
        spread(batch, own_aux, aux, aux_sem, behind)

    def batch_rows(batch):
        return rows[pl.ds(batch * size, size), :]

    def gate_terms(batch):
        await_bytes(rows.at[arrived(batch)], recv_sems.at[rows_sem + batch])
        for j in range(0, parts, 2):
            two = dot(batch_rows(batch), wide[:, j * hidden : (j + 2) * hidden]).astype(BF16)
            partial[batch, j // edge, j % edge] = two[:, :hidden]
            partial[batch, j // edge, j % edge + 1] = two[:, hidden:]

        @pl.loop(1, edge)
        def _(step):
            remote(
                partial.at[batch, :, along(step), first],
                first_terms.at[batch, 0, step - 1],
                first_sem + batch,
                (line * edge + along(step), place),
            )
            remote(
                partial.at[batch, across(step), :, second],
                first_terms.at[batch, 1, step - 1],
                first_sem + batch,
                (across(step) * edge + spot, place),
            )

    def gate_half_sums(batch):
        await_bytes(first_terms.at[batch], recv_sems.at[first_sem + batch])
        one = partial[batch, :, spot, first, :].astype(F32)
        two = partial[batch, line, :, second, :].astype(F32)
        for i in range(edge - 1):
            one = one + first_terms[batch, 0, i].astype(F32)
            two = two + first_terms[batch, 1, i].astype(F32)
        half_sums[batch, 0] = one.astype(BF16)
        half_sums[batch, 1] = two.astype(BF16)

        @pl.loop(1, edge)
        def _(step):
            remote(
                half_sums.at[batch, 0, across(step)],
                second_terms.at[batch, 0, step - 1],
                second_sem + batch,
                (across(step) * edge + spot, place),
            )
            remote(
                half_sums.at[batch, 1, along(step)],
                second_terms.at[batch, 1, step - 1],
                second_sem + batch,
                (line * edge + along(step), place),
            )

    def gate_delta(batch):
        await_bytes(second_terms.at[batch], recv_sems.at[second_sem + batch])
        await_bytes(aux.at[arrived(batch)], recv_sems.at[aux_sem + batch])
        for which, mine, there in ((0, line, first), (1, spot, second)):
            gate = half_sums[batch, which, mine].astype(F32)
            for i in range(edge - 1):
                gate = gate + second_terms[batch, which, i].astype(F32)
            logistic = jax.nn.sigmoid(gate)
            slope = logistic * (1.0 + gate * (1.0 - logistic))
            factor = aux[pl.ds(batch * size + which * half, half), :].astype(F32)
            delta[batch, line, spot, there, :] = (factor * slope).astype(BF16)

        @pl.loop(1, edge)
        def _(step):
            one = delta.at[batch, line, spot, first]
            remote(one, one, third_sem + batch, (across(step) * edge + spot, place))
            two = delta.at[batch, line, spot, second]
            remote(two, two, third_sem + batch, (line * edge + along(step), place))

    def pass_delta(batch):
        await_bytes(second_terms.at[batch], recv_sems.at[third_sem + batch])

        @pl.loop(1, edge)
        def _(step):
            one = delta.at[batch, :, spot, first]
            remote(one, one, fourth_sem + batch, (line * edge + along(step), place))
            two = delta.at[batch, line, :, second]
            remote(two, two, fourth_sem + batch, (across(step) * edge + spot, place))

    def two_parts(batch, j):
        row, column = j // edge, j % edge
        return jnp.concatenate(
            [delta[batch, row, column], delta[batch, row, column + 1]], axis=1
        )

    def route_grads(batch):
        await_bytes(first_terms.at[batch], recv_sems.at[fourth_sem + batch])
        total = jnp.zeros((size, wide.shape[0]), F32)
        for j in range(0, parts, 2):
            columns = wide[:, j * hidden : (j + 2) * hidden]
            total = total + dot(two_parts(batch, j), columns, ((1,), (1,)))
        back[pl.ds(batch * size, size), :] = total.astype(BF16)
        spread(batch, back, ret, ret_sem, ahead)

    def weight_grads(batch):
        turned = batch_rows(batch).T
        for j in range(0, parts, 2):
            there = slice(j * hidden, (j + 2) * hidden)
            two = dot(turned, two_parts(batch, j))
            if batch > 0:
                two = two + totals[:, there]
            if batch < BATCHES - 1:
                totals[:, there] = two
            else:
                grads[j] = two[:share, :hidden].astype(BF16)
                grads[j + 1] = two[:share, hidden:].astype(BF16)

    few = (parts - 1) * share
    await_bytes(weight_ref.at[pl.ds(0, few)], recv_sems.at[weight_sem])
    for batch in range(BATCHES):
        gate_terms(batch)
        if batch > 0:
            pass_delta(batch - 1)
        gate_half_sums(batch)
        if batch > 0:
            route_grads(batch - 1)
            weight_grads(batch - 1)
        gate_delta(batch)
    last = BATCHES - 1
    pass_delta(last)
    route_grads(last)
    weight_grads(last)

    own_share = pl.ds(pl.multiple_of(part * share, 16), share)

    @pl.loop(1, parts)
    def _(step):
        other = lax.rem(part + step, parts)
        remote(grads.at[other], weight_out.at[own_share], grad_sem, (other, place))

    weight_out[own_share, :] = grads[part]

    def hand_over(batch):
        there = pl.ds(batch * size, size)
        await_bytes(ret.at[arrived(batch)], recv_sems.at[ret_sem + batch])
        remote(ret.at[there], twin_ret.at[there], twin_sem + batch, twin)

    for batch in range(BATCHES):
        hand_over(batch)
    total = dot(pick[0], ret[...], ((0,), (0,)))
    for batch in range(BATCHES):
        await_bytes(twin_ret.at[pl.ds(batch * size, size)], recv_sems.at[twin_sem + batch])
    total = total + dot(pick[1], twin_ret[...], ((0,), (0,)))
    token_out[...] = total[:, :share].astype(BF16)

    await_bytes(away_rows, send_sems.at[twin_rows_sem])
    await_bytes(away_aux, send_sems.at[twin_aux_sem])
    await_bytes(weight_ref.at[pl.ds(0, few)], send_sems.at[weight_sem])
    for batch in range(BATCHES):
        await_bytes(rows.at[arrived(batch)], send_sems.at[rows_sem + batch])
        await_bytes(aux.at[arrived(batch)], send_sems.at[aux_sem + batch])
        await_bytes(first_terms.at[batch], send_sems.at[first_sem + batch])
        await_bytes(second_terms.at[batch], send_sems.at[second_sem + batch])
        await_bytes(second_terms.at[batch], send_sems.at[third_sem + batch])
        await_bytes(first_terms.at[batch], send_sems.at[fourth_sem + batch])
        await_bytes(back.at[arrived(batch)], send_sems.at[ret_sem + batch])
        await_bytes(ret.at[pl.ds(batch * size, size)], send_sems.at[twin_sem + batch])
    await_bytes(weight_out.at[pl.ds(0, few)], send_sems.at[grad_sem])
    await_bytes(weight_out.at[pl.ds(0, few)], recv_sems.at[grad_sem])


def local(tokens, up_saved, hidden_grad, route_device, on_replica, gate_weight):
    experts = lax.axis_size("expert")
    parts = lax.axis_size("dp")
    part = lax.axis_index("dp")
    place = lax.axis_index("expert")
    chips = experts // 2
    tok_count, routes = route_device.shape
    width = tokens.shape[1]
    share = width // parts
    padded = -(-share // 128) * 128
    hidden = gate_weight.shape[2]
    slots = chips * PAIR
    size = slots // BATCHES
    edge = math.isqrt(parts)
    tok = lax.dynamic_slice_in_dim(tokens, part * share, share, 1)
    tok = jnp.pad(tok, ((0, 0), (0, padded - share)))
    prod = (hidden_grad.astype(F32) * up_saved.astype(F32)).astype(BF16).transpose(1, 0, 2)
    flag = lax.dynamic_slice_in_dim(on_replica, place, 1, 0).reshape(experts, 1)
    vmem = pl.BlockSpec(memory_space=pltpu.VMEM)
    return pl.pallas_call(
        functools.partial(kernel, parts, chips, share),
        out_shape=(
            jax.ShapeDtypeStruct((tok_count, share), BF16),
            jax.ShapeDtypeStruct((width, hidden), BF16),
        ),
        in_specs=[vmem] * 5,
        out_specs=(vmem, vmem),
        scratch_shapes=[
            pltpu.VMEM((2, slots, tok_count), BF16),
            pltpu.VMEM((slots, padded), BF16),
            pltpu.VMEM((slots, hidden), BF16),
            pltpu.VMEM((slots, padded), BF16),
            pltpu.VMEM((slots, hidden), BF16),
            pltpu.VMEM((slots, padded), BF16),
            pltpu.VMEM((slots, hidden), BF16),
            pltpu.VMEM((slots, padded), BF16),
            pltpu.VMEM((slots, hidden), BF16),
            pltpu.VMEM((padded, parts * hidden), BF16),
            pltpu.VMEM((BATCHES, edge, edge, size, hidden), BF16),
            pltpu.VMEM((BATCHES, 2, edge - 1, edge, size // 2, hidden), BF16),
            pltpu.VMEM((BATCHES, 2, edge, size // 2, hidden), BF16),
            pltpu.VMEM((BATCHES, 2, edge - 1, size // 2, hidden), BF16),
            pltpu.VMEM((BATCHES, edge, edge, size, hidden), BF16),
            pltpu.VMEM((slots, padded), BF16),
            pltpu.VMEM((slots, padded), BF16),
            pltpu.VMEM((slots, padded), BF16),
            pltpu.VMEM((padded, parts * hidden), F32),
            pltpu.VMEM((parts, share, hidden), BF16),
            pltpu.SemaphoreType.DMA((4 + 8 * BATCHES,)),
            pltpu.SemaphoreType.DMA((4 + 8 * BATCHES,)),
        ],
        compiler_params=pltpu.CompilerParams(
            collective_id=0, has_side_effects=True, vmem_limit_bytes=48 * 1024 * 1024
        ),
        cost_estimate=pl.CostEstimate(
            flops=6 * slots * padded * parts * hidden, bytes_accessed=4 << 20, transcendentals=0
        ),
    )(tok, prod, route_device.T, flag, gate_weight[0])


def solution(mesh):
    placed = (
        P("expert", None),
        P("expert", None, "dp"),
        P("expert", None, "dp"),
        P("expert", None),
        P(),
        P("expert", None, "dp"),
    )

    def whole(*args):
        token_grad, gate_grad = local(*args)
        return token_grad, gate_grad[None]

    return jax.shard_map(
        whole,
        mesh=mesh,
        in_specs=placed,
        out_specs=(P("expert", "dp"), P("expert", None, "dp")),
        check_vma=False,
    )
```

```python
import functools
import math

import jax
import jax.numpy as jnp
from jax import lax
from jax.experimental import pallas as pl
from jax.experimental.pallas import tpu as pltpu
from jax.sharding import PartitionSpec as P

CAP = 4
SLOTS = 2 * CAP
PAIR = 2 * SLOTS
BATCHES = 4
SENDS = (
    "r0", "a0", "r3", "r2", "a3", "r1", "a2", "a1",
)
ORDER = (
    "a0", "b0", "c0", "d0", "a3", "a2", "b3", "e0", "a1", "b2",
    "c3", "b1", "d3", "c2", "e3", "d2", "c1", "e2", "d1", "e1",
)
SEQUENCE = [int(step[1:]) for step in ORDER if step[0] == "e"]
MESH = pl.DeviceIdType.MESH
F32 = jnp.float32
BF16 = jnp.bfloat16


def dot(a, b, contract=((1,), (0,))):
    return lax.dot_general(a, b, (contract, ((), ())), preferred_element_type=F32)


def await_bytes(view, sem):
    pltpu.make_async_copy(view, view, sem).wait()


def kernel(
    parts,
    chips,
    share,
    tok_ref,
    prod_ref,
    route_ref,
    flag_ref,
    weight_ref,
    token_out,
    weight_out,
    pick,
    own_rows,
    own_aux,
    away_rows,
    away_aux,
    twin_rows,
    twin_aux,
    rows,
    aux,
    wide,
    partial,
    first_terms,
    half_sums,
    second_terms,
    delta,
    back,
    ret,
    twin_ret,
    totals,
    grads,
    send_sems,
    recv_sems,
):
    experts = 2 * chips
    halfway = experts // 2
    slots = chips * PAIR
    near = chips // BATCHES
    size = slots // BATCHES
    half = size // 2
    edge = half_sums.shape[2]
    tokens = tok_ref.shape[0]
    hidden = prod_ref.shape[2]
    routes = prod_ref.shape[0]
    part = lax.axis_index("dp")
    place = lax.axis_index("expert")
    line, spot = part // edge, part % edge
    chip = place // 2
    core = place % 2
    twin = (part, chip * 2 + 1 - core)
    first, second = pl.ds(0, half), pl.ds(half, half)

    def ahead(step):
        return (part, lax.rem(chip + chips + step, chips) * 2 + core)

    def behind(step):
        return (part, lax.rem(chip + chips - step, chips) * 2 + core)

    def along(step):
        return lax.rem(spot + step, edge)

    def across(step):
        return lax.rem(line + step, edge)

    barrier = pltpu.get_barrier_semaphore()

    def greet(device):
        pl.semaphore_signal(barrier, inc=1, device_id=device, device_id_type=MESH)

    greet(ahead(chips // 2))

    @pl.loop(1, chips // 2)
    def _(step):
        greet(ahead(chips // 2 - step))
        greet(behind(chips // 2 - step))

    @pl.loop(1, parts)
    def _(step):
        greet((lax.rem(part + step, parts), place))

    greet(twin)

    wide[pl.ds(share, wide.shape[0] - share), :] = jnp.zeros(
        (wide.shape[0] - share, wide.shape[1]), BF16
    )

    named = route_ref[...]
    numbers = lax.broadcasted_iota(jnp.int32, (experts, tokens), 0)
    count = jnp.zeros((experts, tokens), F32)
    for k in range(routes):
        count = count + jnp.where(named[k : k + 1, :] == numbers, 1.0, 0.0)
    before = lax.broadcasted_iota(jnp.int32, (tokens, tokens), 0)
    after = lax.broadcasted_iota(jnp.int32, (tokens, tokens), 1)
    earlier = dot(count.astype(BF16), jnp.where(before < after, 1.0, 0.0).astype(BF16))
    flags = flag_ref[...].astype(F32)
    target = []
    for k in range(routes):
        here = named[k : k + 1, :] == numbers
        position = jnp.sum(jnp.where(here, earlier, 0.0), axis=0, keepdims=True).astype(jnp.int32)
        flag = jnp.sum(jnp.where(here, flags, 0.0), axis=0, keepdims=True).astype(jnp.int32)
        number = named[k : k + 1, :]
        server = lax.rem(number + flag * halfway, experts)
        offset = lax.rem(chip + chips + chips // 2 - server // 2, chips) - chips // 2
        rank = jnp.where(offset < 0, -2 * offset - 1, 2 * offset)
        row = rank * PAIR + core * SLOTS + flag * CAP + position
        target.append((jnp.where(number < experts, row, -1), lax.rem(server, 2)))

    row_ids = lax.broadcasted_iota(jnp.int32, (slots, tokens), 0)

    def fill(side, rows_ref, aux_ref):
        total = jnp.zeros((slots, hidden), F32)
        every = jnp.zeros((slots, tokens), F32)
        for k in range(routes):
            row, parity = target[k]
            chosen = jnp.where(row_ids == jnp.where(parity == side, row, -1), 1.0, 0.0)
            every = every + chosen
            total = total + dot(chosen.astype(BF16), prod_ref[k])
        matrix = every.astype(BF16)
        rows_ref[...] = dot(matrix, tok_ref[...]).astype(BF16)
        aux_ref[...] = total.astype(BF16)
        return matrix

    pick[1] = fill(1 - core, away_rows, away_aux)
    pick[0] = fill(core, own_rows, own_aux)
    pl.semaphore_wait(barrier, 1 + (chips - 1) + (parts - 1))

    def remote(src, dst, sem, device):
        copy = pltpu.make_async_remote_copy(
            src_ref=src,
            dst_ref=dst,
            send_sem=send_sems.at[sem],
            recv_sem=recv_sems.at[sem],
            device_id=device,
            device_id_type=MESH,
        )
        copy.start()

    twin_rows_sem, twin_aux_sem, weight_sem, grad_sem = range(4)
    rows_sem, aux_sem, first_sem, second_sem, third_sem, fourth_sem, ret_sem, twin_sem = (
        4 + BATCHES * i for i in range(8)
    )

    remote(away_rows, twin_rows, twin_rows_sem, twin)
    remote(away_aux, twin_aux, twin_aux_sem, twin)

    own_columns = pl.ds(pl.multiple_of(part * hidden, hidden), hidden)

    @pl.loop(1, parts)
    def _(step):
        other = lax.rem(part + step, parts)
        remote(
            weight_ref.at[pl.ds(pl.multiple_of(other * share, 16), share)],
            wide.at[pl.ds(0, share), own_columns],
            weight_sem,
            (other, place),
        )

    wide[pl.ds(0, share), own_columns] = weight_ref[
        pl.ds(pl.multiple_of(part * share, 16), share), :
    ]

    def group(index):
        return pl.ds(pl.multiple_of(index * PAIR, PAIR), PAIR)

    def arrived(batch):
        lowest = batch * size + (PAIR if batch == 0 else 0)
        return pl.ds(lowest, (batch + 1) * size - lowest)

    def spread(batch, src, dst, sem, device_of):
        @pl.loop(0, near - 1 if batch == 0 else near, unroll=True)
        def _(index):
            rank = (batch + 1) * near - 1 - index
            offset = jnp.where(lax.rem(rank, 2) == 1, -((rank + 1) // 2), rank // 2)
            where = group(rank)
            remote(src.at[where], dst.at[where], sem + batch, device_of(offset))

        if batch == 0:
            dst[pl.ds(0, PAIR), :] = src[pl.ds(0, PAIR), :]

    await_bytes(twin_rows, recv_sems.at[twin_rows_sem])
    own_rows[...] = own_rows[...] + twin_rows[...]
    added = False
    for item in SENDS:
        batch = int(item[1:])
        if item[0] == "r":
            spread(batch, own_rows, rows, rows_sem, behind)
            continue
        if not added:
            await_bytes(twin_aux, recv_sems.at[twin_aux_sem])
            own_aux[...] = own_aux[...] + twin_aux[...]
            added = True
        spread(batch, own_aux, aux, aux_sem, behind)

    def batch_rows(batch):
        return rows[pl.ds(batch * size, size), :]

    def gate_terms(batch):
        await_bytes(rows.at[arrived(batch)], recv_sems.at[rows_sem + batch])
        for j in range(0, parts, 2):
            two = dot(batch_rows(batch), wide[:, j * hidden : (j + 2) * hidden]).astype(BF16)
            partial[batch, j // edge, j % edge] = two[:, :hidden]
            partial[batch, j // edge, j % edge + 1] = two[:, hidden:]

        @pl.loop(1, edge, unroll=True)
        def _(step):
            remote(
                partial.at[batch, :, along(step), first],
                first_terms.at[batch, 0, step - 1],
                first_sem + batch,
                (line * edge + along(step), place),
            )
            remote(
                partial.at[batch, across(step), :, second],
                first_terms.at[batch, 1, step - 1],
                first_sem + batch,
                (across(step) * edge + spot, place),
            )

    def gate_half_sums(batch):
        await_bytes(first_terms.at[batch], recv_sems.at[first_sem + batch])
        one = partial[batch, :, spot, first, :].astype(F32)
        two = partial[batch, line, :, second, :].astype(F32)
        for i in range(edge - 1):
            one = one + first_terms[batch, 0, i].astype(F32)
            two = two + first_terms[batch, 1, i].astype(F32)
        half_sums[batch, 0] = one.astype(BF16)
        half_sums[batch, 1] = two.astype(BF16)

        @pl.loop(1, edge, unroll=True)
        def _(step):
            remote(
                half_sums.at[batch, 0, across(step)],
                second_terms.at[batch, 0, step - 1],
                second_sem + batch,
                (across(step) * edge + spot, place),
            )
            remote(
                half_sums.at[batch, 1, along(step)],
                second_terms.at[batch, 1, step - 1],
                second_sem + batch,
                (line * edge + along(step), place),
            )

    def gate_delta(batch):
        await_bytes(second_terms.at[batch], recv_sems.at[second_sem + batch])
        await_bytes(aux.at[arrived(batch)], recv_sems.at[aux_sem + batch])
        for which, mine, there in ((0, line, first), (1, spot, second)):
            gate = half_sums[batch, which, mine].astype(F32)
            for i in range(edge - 1):
                gate = gate + second_terms[batch, which, i].astype(F32)
            logistic = jax.nn.sigmoid(gate)
            slope = logistic * (1.0 + gate * (1.0 - logistic))
            factor = aux[pl.ds(batch * size + which * half, half), :].astype(F32)
            delta[batch, line, spot, there, :] = (factor * slope).astype(BF16)

        @pl.loop(1, edge, unroll=True)
        def _(step):
            one = delta.at[batch, line, spot, first]
            remote(one, one, third_sem + batch, (across(step) * edge + spot, place))
            two = delta.at[batch, line, spot, second]
            remote(two, two, third_sem + batch, (line * edge + along(step), place))

    def pass_delta(batch):
        await_bytes(second_terms.at[batch], recv_sems.at[third_sem + batch])

        @pl.loop(1, edge, unroll=True)
        def _(step):
            one = delta.at[batch, :, spot, first]
            remote(one, one, fourth_sem + batch, (line * edge + along(step), place))
            two = delta.at[batch, line, :, second]
            remote(two, two, fourth_sem + batch, (across(step) * edge + spot, place))

    def two_parts(batch, j):
        row, column = j // edge, j % edge
        return jnp.concatenate(
            [delta[batch, row, column], delta[batch, row, column + 1]], axis=1
        )

    def route_grads(batch):
        total = jnp.zeros((size, wide.shape[0]), F32)
        for j in range(0, parts, 2):
            columns = wide[:, j * hidden : (j + 2) * hidden]
            total = total + dot(two_parts(batch, j), columns, ((1,), (1,)))
        back[pl.ds(batch * size, size), :] = total.astype(BF16)
        spread(batch, back, ret, ret_sem, ahead)

    def weight_grads(batch):
        turned = batch_rows(batch).T
        for j in range(0, parts, 2):
            there = slice(j * hidden, (j + 2) * hidden)
            two = dot(turned, two_parts(batch, j))
            if batch != SEQUENCE[0]:
                two = two + totals[:, there]
            if batch != SEQUENCE[-1]:
                totals[:, there] = two
            else:
                grads[j] = two[:share, :hidden].astype(BF16)
                grads[j + 1] = two[:share, hidden:].astype(BF16)

    few = (parts - 1) * share
    await_bytes(weight_ref.at[pl.ds(0, few)], recv_sems.at[weight_sem])
    own_share = pl.ds(pl.multiple_of(part * share, 16), share)

    def send_weight_grads():
        @pl.loop(1, parts)
        def _(step):
            other = lax.rem(part + step, parts)
            remote(grads.at[other], weight_out.at[own_share], grad_sem, (other, place))

        weight_out[own_share, :] = grads[part]

    def close(batch):
        await_bytes(first_terms.at[batch], recv_sems.at[fourth_sem + batch])
        if batch == SEQUENCE[-1]:
            weight_grads(batch)
            send_weight_grads()
            route_grads(batch)
        else:
            route_grads(batch)
            weight_grads(batch)

    stages = dict(a=gate_terms, b=gate_half_sums, c=gate_delta, d=pass_delta, e=close)
    for step in ORDER:
        stages[step[0]](int(step[1:]))

    def hand_over(batch):
        there = pl.ds(batch * size, size)
        await_bytes(ret.at[arrived(batch)], recv_sems.at[ret_sem + batch])
        remote(ret.at[there], twin_ret.at[there], twin_sem + batch, twin)

    for batch in SEQUENCE:
        hand_over(batch)
    total = dot(pick[0], ret[...], ((0,), (0,)))
    for batch in range(BATCHES):
        await_bytes(twin_ret.at[pl.ds(batch * size, size)], recv_sems.at[twin_sem + batch])
    total = total + dot(pick[1], twin_ret[...], ((0,), (0,)))
    token_out[...] = total[:, :share].astype(BF16)

    await_bytes(away_rows, send_sems.at[twin_rows_sem])
    await_bytes(away_aux, send_sems.at[twin_aux_sem])
    await_bytes(weight_ref.at[pl.ds(0, few)], send_sems.at[weight_sem])
    for batch in range(BATCHES):
        await_bytes(rows.at[arrived(batch)], send_sems.at[rows_sem + batch])
        await_bytes(aux.at[arrived(batch)], send_sems.at[aux_sem + batch])
        await_bytes(first_terms.at[batch], send_sems.at[first_sem + batch])
        await_bytes(second_terms.at[batch], send_sems.at[second_sem + batch])
        await_bytes(second_terms.at[batch], send_sems.at[third_sem + batch])
        await_bytes(first_terms.at[batch], send_sems.at[fourth_sem + batch])
        await_bytes(back.at[arrived(batch)], send_sems.at[ret_sem + batch])
        await_bytes(ret.at[pl.ds(batch * size, size)], send_sems.at[twin_sem + batch])
    await_bytes(weight_out.at[pl.ds(0, few)], send_sems.at[grad_sem])
    await_bytes(weight_out.at[pl.ds(0, few)], recv_sems.at[grad_sem])


def local(tokens, up_saved, hidden_grad, route_device, on_replica, gate_weight):
    experts = lax.axis_size("expert")
    parts = lax.axis_size("dp")
    part = lax.axis_index("dp")
    place = lax.axis_index("expert")
    chips = experts // 2
    tok_count, routes = route_device.shape
    width = tokens.shape[1]
    share = width // parts
    padded = -(-share // 128) * 128
    hidden = gate_weight.shape[2]
    slots = chips * PAIR
    size = slots // BATCHES
    edge = math.isqrt(parts)
    tok = lax.dynamic_slice_in_dim(tokens, part * share, share, 1)
    tok = jnp.pad(tok, ((0, 0), (0, padded - share)))
    prod = (hidden_grad.astype(F32) * up_saved.astype(F32)).astype(BF16).transpose(1, 0, 2)
    flag = lax.dynamic_slice_in_dim(on_replica, place, 1, 0).reshape(experts, 1)
    vmem = pl.BlockSpec(memory_space=pltpu.VMEM)
    return pl.pallas_call(
        functools.partial(kernel, parts, chips, share),
        out_shape=(
            jax.ShapeDtypeStruct((tok_count, share), BF16),
            jax.ShapeDtypeStruct((width, hidden), BF16),
        ),
        in_specs=[vmem] * 5,
        out_specs=(vmem, vmem),
        scratch_shapes=[
            pltpu.VMEM((2, slots, tok_count), BF16),
            pltpu.VMEM((slots, padded), BF16),
            pltpu.VMEM((slots, hidden), BF16),
            pltpu.VMEM((slots, padded), BF16),
            pltpu.VMEM((slots, hidden), BF16),
            pltpu.VMEM((slots, padded), BF16),
            pltpu.VMEM((slots, hidden), BF16),
            pltpu.VMEM((slots, padded), BF16),
            pltpu.VMEM((slots, hidden), BF16),
            pltpu.VMEM((padded, parts * hidden), BF16),
            pltpu.VMEM((BATCHES, edge, edge, size, hidden), BF16),
            pltpu.VMEM((BATCHES, 2, edge - 1, edge, size // 2, hidden), BF16),
            pltpu.VMEM((BATCHES, 2, edge, size // 2, hidden), BF16),
            pltpu.VMEM((BATCHES, 2, edge - 1, size // 2, hidden), BF16),
            pltpu.VMEM((BATCHES, edge, edge, size, hidden), BF16),
            pltpu.VMEM((slots, padded), BF16),
            pltpu.VMEM((slots, padded), BF16),
            pltpu.VMEM((slots, padded), BF16),
            pltpu.VMEM((padded, parts * hidden), F32),
            pltpu.VMEM((parts, share, hidden), BF16),
            pltpu.SemaphoreType.DMA((4 + 8 * BATCHES,)),
            pltpu.SemaphoreType.DMA((4 + 8 * BATCHES,)),
        ],
        compiler_params=pltpu.CompilerParams(
            collective_id=0, has_side_effects=True, vmem_limit_bytes=48 * 1024 * 1024
        ),
        cost_estimate=pl.CostEstimate(
            flops=6 * slots * padded * parts * hidden, bytes_accessed=4 << 20, transcendentals=0
        ),
    )(tok, prod, route_device.T, flag, gate_weight[0])


def solution(mesh):
    placed = (
        P("expert", None),
        P("expert", None, "dp"),
        P("expert", None, "dp"),
        P("expert", None),
        P(),
        P("expert", None, "dp"),
    )

    def whole(*args):
        token_grad, gate_grad = local(*args)
        return token_grad, gate_grad[None]

    return jax.shard_map(
        whole,
        mesh=mesh,
        in_specs=placed,
        out_specs=(P("expert", "dp"), P("expert", None, "dp")),
        check_vma=False,
    )
```

```python
import functools
import math

import jax
import jax.numpy as jnp
from jax import lax
from jax.experimental import pallas as pl
from jax.experimental.pallas import tpu as pltpu
from jax.sharding import PartitionSpec as P

CAP = 4
SLOTS = 2 * CAP
PAIR = 2 * SLOTS
BATCHES = 4
SENDS = (
    "r0", "a0", "r3", "r2", "a3", "r1", "a2", "a1",
)
ORDER = (
    "a0", "b0", "c0", "a3", "d0", "a2", "b3", "e0", "w0", "a1", "b2",
    "c3", "b1", "d3", "c2", "c1", "d2", "e3", "d1", "w3", "e2", "w2", "e1",
)
SEQUENCE = [int(step[1:]) for step in ORDER if step[0] == "e"]
MESH = pl.DeviceIdType.MESH
F32 = jnp.float32
BF16 = jnp.bfloat16


def dot(a, b, contract=((1,), (0,))):
    return lax.dot_general(a, b, (contract, ((), ())), preferred_element_type=F32)


def await_bytes(view, sem):
    pltpu.make_async_copy(view, view, sem).wait()


def kernel(
    parts,
    chips,
    share,
    tok_ref,
    prod_ref,
    route_ref,
    flag_ref,
    weight_ref,
    token_out,
    weight_out,
    pick,
    own_rows,
    own_aux,
    away_rows,
    away_aux,
    twin_rows,
    twin_aux,
    rows,
    aux,
    wide,
    partial,
    first_terms,
    half_sums,
    second_terms,
    delta,
    back,
    ret,
    twin_ret,
    totals,
    grads,
    send_sems,
    recv_sems,
):
    experts = 2 * chips
    halfway = experts // 2
    slots = chips * PAIR
    near = chips // BATCHES
    size = slots // BATCHES
    half = size // 2
    edge = half_sums.shape[2]
    tokens = tok_ref.shape[0]
    hidden = prod_ref.shape[2]
    routes = prod_ref.shape[0]
    part = lax.axis_index("dp")
    place = lax.axis_index("expert")
    line, spot = part // edge, part % edge
    chip = place // 2
    core = place % 2
    twin = (part, chip * 2 + 1 - core)
    first, second = pl.ds(0, half), pl.ds(half, half)

    def ahead(step):
        return (part, lax.rem(chip + chips + step, chips) * 2 + core)

    def behind(step):
        return (part, lax.rem(chip + chips - step, chips) * 2 + core)

    def along(step):
        return lax.rem(spot + step, edge)

    def across(step):
        return lax.rem(line + step, edge)

    barrier = pltpu.get_barrier_semaphore()

    def greet(device):
        pl.semaphore_signal(barrier, inc=1, device_id=device, device_id_type=MESH)

    greet(ahead(chips // 2))

    @pl.loop(1, chips // 2, unroll=True)
    def _(step):
        greet(ahead(chips // 2 - step))
        greet(behind(chips // 2 - step))

    @pl.loop(1, parts, unroll=True)
    def _(step):
        greet((lax.rem(part + step, parts), place))

    greet(twin)

    wide[pl.ds(share, wide.shape[0] - share), :] = jnp.zeros(
        (wide.shape[0] - share, wide.shape[1]), BF16
    )

    named = route_ref[...]
    numbers = lax.broadcasted_iota(jnp.int32, (experts, tokens), 0)
    count = jnp.zeros((experts, tokens), F32)
    for k in range(routes):
        count = count + jnp.where(named[k : k + 1, :] == numbers, 1.0, 0.0)
    before = lax.broadcasted_iota(jnp.int32, (tokens, tokens), 0)
    after = lax.broadcasted_iota(jnp.int32, (tokens, tokens), 1)
    earlier = dot(count.astype(BF16), jnp.where(before < after, 1.0, 0.0).astype(BF16))
    flags = flag_ref[...].astype(F32)
    target = []
    for k in range(routes):
        here = named[k : k + 1, :] == numbers
        position = jnp.sum(jnp.where(here, earlier, 0.0), axis=0, keepdims=True).astype(jnp.int32)
        flag = jnp.sum(jnp.where(here, flags, 0.0), axis=0, keepdims=True).astype(jnp.int32)
        number = named[k : k + 1, :]
        server = lax.rem(number + flag * halfway, experts)
        offset = lax.rem(chip + chips + chips // 2 - server // 2, chips) - chips // 2
        rank = jnp.where(offset < 0, -2 * offset - 1, 2 * offset)
        row = rank * PAIR + core * SLOTS + flag * CAP + position
        target.append((jnp.where(number < experts, row, -1), lax.rem(server, 2)))

    row_ids = lax.broadcasted_iota(jnp.int32, (slots, tokens), 0)

    def fill(side, rows_ref, aux_ref):
        total = jnp.zeros((slots, hidden), F32)
        every = jnp.zeros((slots, tokens), F32)
        for k in range(routes):
            row, parity = target[k]
            chosen = jnp.where(row_ids == jnp.where(parity == side, row, -1), 1.0, 0.0)
            every = every + chosen
            total = total + dot(chosen.astype(BF16), prod_ref[k])
        matrix = every.astype(BF16)
        rows_ref[...] = dot(matrix, tok_ref[...]).astype(BF16)
        aux_ref[...] = total.astype(BF16)
        return matrix

    pick[1] = fill(1 - core, away_rows, away_aux)
    pl.semaphore_wait(barrier, 1 + (chips - 1) + (parts - 1))

    def remote(src, dst, sem, device):
        copy = pltpu.make_async_remote_copy(
            src_ref=src,
            dst_ref=dst,
            send_sem=send_sems.at[sem],
            recv_sem=recv_sems.at[sem],
            device_id=device,
            device_id_type=MESH,
        )
        copy.start()

    twin_rows_sem, twin_aux_sem, weight_sem, grad_sem = range(4)
    rows_sem, aux_sem, first_sem, second_sem, third_sem, fourth_sem, ret_sem, twin_sem = (
        4 + BATCHES * i for i in range(8)
    )

    remote(away_rows, twin_rows, twin_rows_sem, twin)
    remote(away_aux, twin_aux, twin_aux_sem, twin)

    own_columns = pl.ds(pl.multiple_of(part * hidden, hidden), hidden)

    @pl.loop(1, parts)
    def _(step):
        other = lax.rem(part + step, parts)
        remote(
            weight_ref.at[pl.ds(pl.multiple_of(other * share, 16), share)],
            wide.at[pl.ds(0, share), own_columns],
            weight_sem,
            (other, place),
        )

    wide[pl.ds(0, share), own_columns] = weight_ref[
        pl.ds(pl.multiple_of(part * share, 16), share), :
    ]

    pick[0] = fill(core, own_rows, own_aux)

    def group(index):
        return pl.ds(pl.multiple_of(index * PAIR, PAIR), PAIR)

    def arrived(batch):
        lowest = batch * size + (PAIR if batch == 0 else 0)
        return pl.ds(lowest, (batch + 1) * size - lowest)

    def spread(batch, src, dst, sem, device_of):
        @pl.loop(0, near - 1 if batch == 0 else near, unroll=True)
        def _(index):
            rank = (batch + 1) * near - 1 - index
            offset = jnp.where(lax.rem(rank, 2) == 1, -((rank + 1) // 2), rank // 2)
            where = group(rank)
            remote(src.at[where], dst.at[where], sem + batch, device_of(offset))

        if batch == 0:
            dst[pl.ds(0, PAIR), :] = src[pl.ds(0, PAIR), :]

    await_bytes(twin_rows, recv_sems.at[twin_rows_sem])
    own_rows[...] = own_rows[...] + twin_rows[...]
    added = False
    for item in SENDS:
        batch = int(item[1:])
        if item[0] == "r":
            spread(batch, own_rows, rows, rows_sem, behind)
            continue
        if not added:
            await_bytes(twin_aux, recv_sems.at[twin_aux_sem])
            own_aux[...] = own_aux[...] + twin_aux[...]
            added = True
        spread(batch, own_aux, aux, aux_sem, behind)

    def batch_rows(batch):
        return rows[pl.ds(batch * size, size), :]

    def gate_terms(batch):
        await_bytes(rows.at[arrived(batch)], recv_sems.at[rows_sem + batch])
        for j in range(0, parts, 2):
            two = dot(batch_rows(batch), wide[:, j * hidden : (j + 2) * hidden]).astype(BF16)
            partial[batch, j // edge, j % edge] = two[:, :hidden]
            partial[batch, j // edge, j % edge + 1] = two[:, hidden:]

        @pl.loop(1, edge, unroll=True)
        def _(step):
            remote(
                partial.at[batch, :, along(step), first],
                first_terms.at[batch, 0, step - 1],
                first_sem + batch,
                (line * edge + along(step), place),
            )
            remote(
                partial.at[batch, across(step), :, second],
                first_terms.at[batch, 1, step - 1],
                first_sem + batch,
                (across(step) * edge + spot, place),
            )

    def gate_half_sums(batch):
        await_bytes(first_terms.at[batch], recv_sems.at[first_sem + batch])
        one = partial[batch, :, spot, first, :].astype(F32)
        two = partial[batch, line, :, second, :].astype(F32)
        for i in range(edge - 1):
            one = one + first_terms[batch, 0, i].astype(F32)
            two = two + first_terms[batch, 1, i].astype(F32)
        half_sums[batch, 0] = one.astype(BF16)
        half_sums[batch, 1] = two.astype(BF16)

        @pl.loop(1, edge, unroll=True)
        def _(step):
            remote(
                half_sums.at[batch, 0, across(step)],
                second_terms.at[batch, 0, step - 1],
                second_sem + batch,
                (across(step) * edge + spot, place),
            )
            remote(
                half_sums.at[batch, 1, along(step)],
                second_terms.at[batch, 1, step - 1],
                second_sem + batch,
                (line * edge + along(step), place),
            )

    def gate_delta(batch):
        await_bytes(second_terms.at[batch], recv_sems.at[second_sem + batch])
        await_bytes(aux.at[arrived(batch)], recv_sems.at[aux_sem + batch])
        for which, mine, there in ((0, line, first), (1, spot, second)):
            gate = half_sums[batch, which, mine].astype(F32)
            for i in range(edge - 1):
                gate = gate + second_terms[batch, which, i].astype(F32)
            logistic = jax.nn.sigmoid(gate)
            slope = logistic * (1.0 + gate * (1.0 - logistic))
            factor = aux[pl.ds(batch * size + which * half, half), :].astype(F32)
            delta[batch, line, spot, there, :] = (factor * slope).astype(BF16)

        @pl.loop(1, edge, unroll=True)
        def _(step):
            one = delta.at[batch, line, spot, first]
            remote(one, one, third_sem + batch, (across(step) * edge + spot, place))
            two = delta.at[batch, line, spot, second]
            remote(two, two, third_sem + batch, (line * edge + along(step), place))

    def pass_delta(batch):
        await_bytes(second_terms.at[batch], recv_sems.at[third_sem + batch])

        @pl.loop(1, edge, unroll=True)
        def _(step):
            one = delta.at[batch, :, spot, first]
            remote(one, one, fourth_sem + batch, (line * edge + along(step), place))
            two = delta.at[batch, line, :, second]
            remote(two, two, fourth_sem + batch, (across(step) * edge + spot, place))

    def two_parts(batch, j):
        row, column = j // edge, j % edge
        return jnp.concatenate(
            [delta[batch, row, column], delta[batch, row, column + 1]], axis=1
        )

    def route_grads(batch):
        total = jnp.zeros((size, wide.shape[0]), F32)
        for j in range(0, parts, 2):
            columns = wide[:, j * hidden : (j + 2) * hidden]
            total = total + dot(two_parts(batch, j), columns, ((1,), (1,)))
        back[pl.ds(batch * size, size), :] = total.astype(BF16)
        spread(batch, back, ret, ret_sem, ahead)

    own_share = pl.ds(pl.multiple_of(part * share, 16), share)

    def weight_grads(batch):
        turned = batch_rows(batch).T
        for j in range(0, parts, 2):
            there = slice(j * hidden, (j + 2) * hidden)
            two = dot(turned, two_parts(batch, j))
            totals[:, there] = two if batch == SEQUENCE[0] else two + totals[:, there]

    def last_weight_grads(batch):
        turned = batch_rows(batch).T

        @pl.loop(0, parts // 2)
        def _(step):
            j = 2 * lax.rem(part // 2 + step, parts // 2)
            there = pl.ds(pl.multiple_of(j * hidden, 2 * hidden), 2 * hidden)
            two = dot(turned, two_parts(batch, j)) + totals[:, there]
            grads[j] = two[:share, :hidden].astype(BF16)
            grads[j + 1] = two[:share, hidden:].astype(BF16)
            for i in range(2):

                @pl.when(j + i != part)
                def _(other=j + i):
                    remote(grads.at[other], weight_out.at[own_share], grad_sem, (other, place))

        weight_out[own_share, :] = grads[part]

    def finish(batch):
        await_bytes(first_terms.at[batch], recv_sems.at[fourth_sem + batch])
        if batch == SEQUENCE[-1]:
            last_weight_grads(batch)
        route_grads(batch)

    few = (parts - 1) * share
    await_bytes(weight_ref.at[pl.ds(0, few)], recv_sems.at[weight_sem])
    stages = dict(a=gate_terms, b=gate_half_sums, c=gate_delta, d=pass_delta, e=finish, w=weight_grads)
    for step in ORDER:
        stages[step[0]](int(step[1:]))

    def hand_over(batch):
        there = pl.ds(batch * size, size)
        await_bytes(ret.at[arrived(batch)], recv_sems.at[ret_sem + batch])
        remote(ret.at[there], twin_ret.at[there], twin_sem + batch, twin)

    for batch in SEQUENCE:
        hand_over(batch)
    total = dot(ret[...], pick[0], ((0,), (0,)))
    for batch in range(BATCHES):
        await_bytes(twin_ret.at[pl.ds(batch * size, size)], recv_sems.at[twin_sem + batch])
    total = total + dot(twin_ret[...], pick[1], ((0,), (0,)))
    token_out[...] = total[:share].astype(BF16)

    await_bytes(away_rows, send_sems.at[twin_rows_sem])
    await_bytes(away_aux, send_sems.at[twin_aux_sem])
    await_bytes(weight_ref.at[pl.ds(0, few)], send_sems.at[weight_sem])
    for batch in range(BATCHES):
        await_bytes(rows.at[arrived(batch)], send_sems.at[rows_sem + batch])
        await_bytes(aux.at[arrived(batch)], send_sems.at[aux_sem + batch])
        await_bytes(first_terms.at[batch], send_sems.at[first_sem + batch])
        await_bytes(second_terms.at[batch], send_sems.at[second_sem + batch])
        await_bytes(second_terms.at[batch], send_sems.at[third_sem + batch])
        await_bytes(first_terms.at[batch], send_sems.at[fourth_sem + batch])
        await_bytes(back.at[arrived(batch)], send_sems.at[ret_sem + batch])
        await_bytes(ret.at[pl.ds(batch * size, size)], send_sems.at[twin_sem + batch])
    await_bytes(weight_out.at[pl.ds(0, few)], send_sems.at[grad_sem])
    await_bytes(weight_out.at[pl.ds(0, few)], recv_sems.at[grad_sem])


def local(tokens, up_saved, hidden_grad, route_device, on_replica, gate_weight):
    experts = lax.axis_size("expert")
    parts = lax.axis_size("dp")
    part = lax.axis_index("dp")
    place = lax.axis_index("expert")
    chips = experts // 2
    tok_count, routes = route_device.shape
    width = tokens.shape[1]
    share = width // parts
    padded = -(-share // 128) * 128
    hidden = gate_weight.shape[2]
    slots = chips * PAIR
    size = slots // BATCHES
    edge = math.isqrt(parts)
    tok = lax.dynamic_slice_in_dim(tokens, part * share, share, 1)
    tok = jnp.pad(tok, ((0, 0), (0, padded - share)))
    prod = (hidden_grad.astype(F32) * up_saved.astype(F32)).astype(BF16).transpose(1, 0, 2)
    flag = lax.dynamic_slice_in_dim(on_replica, place, 1, 0).reshape(experts, 1)
    vmem = pl.BlockSpec(memory_space=pltpu.VMEM)
    return pl.pallas_call(
        functools.partial(kernel, parts, chips, share),
        out_shape=(
            jax.ShapeDtypeStruct((share, tok_count), BF16),
            jax.ShapeDtypeStruct((width, hidden), BF16),
        ),
        in_specs=[vmem] * 5,
        out_specs=(vmem, vmem),
        scratch_shapes=[
            pltpu.VMEM((2, slots, tok_count), BF16),
            pltpu.VMEM((slots, padded), BF16),
            pltpu.VMEM((slots, hidden), BF16),
            pltpu.VMEM((slots, padded), BF16),
            pltpu.VMEM((slots, hidden), BF16),
            pltpu.VMEM((slots, padded), BF16),
            pltpu.VMEM((slots, hidden), BF16),
            pltpu.VMEM((slots, padded), BF16),
            pltpu.VMEM((slots, hidden), BF16),
            pltpu.VMEM((padded, parts * hidden), BF16),
            pltpu.VMEM((BATCHES, edge, edge, size, hidden), BF16),
            pltpu.VMEM((BATCHES, 2, edge - 1, edge, size // 2, hidden), BF16),
            pltpu.VMEM((BATCHES, 2, edge, size // 2, hidden), BF16),
            pltpu.VMEM((BATCHES, 2, edge - 1, size // 2, hidden), BF16),
            pltpu.VMEM((BATCHES, edge, edge, size, hidden), BF16),
            pltpu.VMEM((slots, padded), BF16),
            pltpu.VMEM((slots, padded), BF16),
            pltpu.VMEM((slots, padded), BF16),
            pltpu.VMEM((padded, parts * hidden), F32),
            pltpu.VMEM((parts, share, hidden), BF16),
            pltpu.SemaphoreType.DMA((4 + 8 * BATCHES,)),
            pltpu.SemaphoreType.DMA((4 + 8 * BATCHES,)),
        ],
        compiler_params=pltpu.CompilerParams(
            collective_id=0, has_side_effects=True, vmem_limit_bytes=48 * 1024 * 1024
        ),
        cost_estimate=pl.CostEstimate(
            flops=6 * slots * padded * parts * hidden, bytes_accessed=4 << 20, transcendentals=0
        ),
    )(tok, prod, route_device.T, flag, gate_weight[0])


def solution(mesh):
    placed = (
        P("expert", None),
        P("expert", None, "dp"),
        P("expert", None, "dp"),
        P("expert", None),
        P(),
        P("expert", None, "dp"),
    )

    def whole(*args):
        token_grad, gate_grad = local(*args)
        return token_grad.T, gate_grad[None]

    return jax.shard_map(
        whole,
        mesh=mesh,
        in_specs=placed,
        out_specs=(P("expert", "dp"), P("expert", None, "dp")),
        check_vma=False,
    )
```
